32 devices in a mesh: loop: 4 (over y, x), grp: 8 (over z, core).
Axes of the slice: x: 2, y: 2, z: 4, core: 2. Of those that a mesh axis runs over, the one named last changes fastest.
Arguments:
- queries: bfloat16 [512, 1024], P(('loop', 'grp')), may hold values from -100 to 100
- landmarks: bfloat16 [2048, 1024], P(('loop', 'grp')), may hold values from -20 to 20
- labels: bfloat16 [2048, 128], P(('loop', 'grp')), may hold values from -6 to 6
- tile_mask: int32 [4, 32], replicated, may hold values from 0 to 1, as said below
Outputs:
- label_scores: bfloat16 [512, 128], P(('loop', 'grp'))
The draws below stay inside these ranges and needn't reach their ends.
Inputs may be any that keep to these rules, and one draw needn't show every extreme that they name: `tile_mask`: every query tile lists at least one landmark tile.
All inputs are finite; a program needn't handle non-finite values.
Results may differ from the reference program's by a relative error of at most 0.0065.
Values may be sent and summed in bfloat16 or wider, within the bound.
A program may use at most 64 MiB of HBM per device.

```python
import math
import jax
import jax.numpy as jnp
from jax import lax

D = 1024
C = 128
LDEV = 64
Q_TILE = 128
Q_TILES = 4
QUERIES = 512
L_TILES = 32
LANDMARKS = 2048


def tile_lists(key):
    base_key = jax.random.fold_in(key, 11)
    key_rate = jax.random.fold_in(base_key, 1)
    key_bits = jax.random.fold_in(base_key, 2)
    key_pick = jax.random.fold_in(base_key, 3)
    threshold = jax.random.randint(key_rate, (Q_TILES, 1), 2, 33)
    draw_bits = jax.random.randint(key_bits, (Q_TILES, L_TILES), 0, 64)
    forced = jax.random.randint(key_pick, (Q_TILES,), 0, L_TILES)
    tile_ids = jnp.arange(L_TILES, dtype=jnp.int32)
    listed = (draw_bits < threshold) | (tile_ids[None, :] == forced[:, None])
    return (listed.astype(jnp.int32), forced)


def tile_strength(tile_ids):
    phase = tile_ids % 3
    target = jnp.where(phase == 0, 220.0, jnp.where(phase == 1, 320.0, 420.0)).astype(jnp.float32)
    return 0.5 + target / (4.0 * math.sqrt(D))


def landmark_rows(key):
    land_key = jax.random.fold_in(key, 31)
    values = jnp.clip(jax.random.normal(land_key, (LANDMARKS, D), jnp.float32), -6.0, 6.0)
    tile_ids = jnp.arange(L_TILES, dtype=jnp.int32)
    strength = tile_strength(tile_ids)
    stretch = 2.0 / (4.0 * math.sqrt(D) * (strength - 1.0))
    first_rows = values[tile_ids * LDEV]
    values = values.at[tile_ids * LDEV + 1].set(first_rows * (1.0 + stretch)[:, None])
    return values


def draw_tile_mask(key, part):
    listed, forced = tile_lists(key)
    return listed


def draw_landmarks(key, part):
    return landmark_rows(key).astype(jnp.bfloat16)


def draw_queries(key, part):
    query_key = jax.random.fold_in(key, 21)
    values = jnp.clip(jax.random.normal(query_key, (QUERIES, D), jnp.float32), -6.0, 6.0)
    listed, forced = tile_lists(key)
    land_values = landmark_rows(key).astype(jnp.bfloat16).astype(jnp.float32)
    strength = tile_strength(forced)
    targets = land_values[forced * LDEV] * strength[:, None]
    values = values.at[jnp.arange(Q_TILES, dtype=jnp.int32) * Q_TILE].set(targets)
    return values.astype(jnp.bfloat16)


def levels(key, extent, pieces, least, high):
    factor_of, own = 1.0, jax.random.fold_in(key, 6)
    for dim, shards_of in pieces:
        draws = jnp.exp(jax.random.uniform(jax.random.fold_in(own, dim), (shards_of,), jnp.float32, least / len(pieces), high / len(pieces)))
        factor_of = factor_of * jnp.repeat(draws, extent[dim] // shards_of).reshape([-1 if axis == dim else 1 for axis in range(len(extent))])
    return factor_of


def scatter_about(own_key, shape, deviation, limit, cuts=(), held_as=jnp.bfloat16):
    result = jax.random.normal(own_key, shape, jnp.float32) * deviation
    if len(cuts) > 0:
        result = levels(own_key, shape, cuts, -0.22, 0.18) * result
    return jnp.clip(result, min=-limit, max=limit).astype(held_as)


def setup_inputs(seed: int = 0) -> dict:
    key_of = jax.random.split(jax.random.key(seed), 5)
    return {
        "queries": draw_queries(jax.random.fold_in(key_of[4], 71), 0),
        "landmarks": draw_landmarks(jax.random.fold_in(key_of[4], 71), 0),
        "labels": scatter_about(key_of[2], (LANDMARKS, C), 1.0, 6.0, ((0, 32),)),
        "tile_mask": draw_tile_mask(jax.random.fold_in(key_of[4], 71), 0),
    }


def reference(queries, landmarks, labels, tile_mask):
    scale_factor = 4.0 / math.sqrt(D)
    land_f = landmarks.astype(jnp.float32)
    half_norm = 0.5 * lax.optimization_barrier(jnp.sum(land_f * land_f, axis=1))
    listed = jnp.repeat(tile_mask, LDEV, axis=1) > 0
    query_tiles = queries.reshape(Q_TILES, Q_TILE, D)

    def per_tile(tile_args):
        query_slab, listed_row = tile_args
        logits = lax.dot_general(query_slab, landmarks, (((1,), (1,)), ((), ())), preferred_element_type=jnp.float32)
        logits = (logits - half_norm[None, :]) * scale_factor
        masked = jnp.where(listed_row[None, :], logits, jnp.float32(-1e+30))
        row_max = lax.optimization_barrier(jnp.max(masked, axis=1, keepdims=True))
        kernel = jnp.where(listed_row[None, :], jnp.exp(logits - row_max), jnp.float32(0.0))
        weight_sum = lax.optimization_barrier(jnp.sum(kernel, axis=1))
        label_sum = jnp.dot(kernel.astype(jnp.bfloat16), labels, preferred_element_type=jnp.float32)
        return (label_sum / weight_sum[:, None]).astype(jnp.bfloat16)
    scores_out = lax.map(per_tile, (query_tiles, listed))
    return scores_out.reshape(QUERIES, C)
```

```python
import functools
import math

import jax
import jax.numpy as jnp
from jax import lax
from jax.experimental import pallas as pl
from jax.experimental.pallas import tpu as pltpu
from jax.sharding import PartitionSpec as P

MESH = pl.DeviceIdType.MESH
CHUNKS = 2


def three_terms(value):
    first = value.astype(jnp.bfloat16)
    rest = value - first.astype(jnp.float32)
    second = rest.astype(jnp.bfloat16)
    third = (rest - second.astype(jnp.float32)).astype(jnp.bfloat16)
    return [t.astype(jnp.float32) for t in (first, second, third)]


def kernel(
    dims,
    mask_ref,
    q_hbm,
    land_hbm,
    lab_hbm,
    out_ref,
    q_all,
    land_all,
    lab_all,
    part,
    got,
    own_sem,
    qz_send,
    qz_recv,
    qy_send,
    qy_recv,
    lx_send,
    lx_recv,
    bx_send,
    bx_recv,
    ls_send,
    ls_recv,
    bs_send,
    bs_recv,
    p_send,
    p_recv,
):
    n_hi, n_lo, n_z, n_core = dims
    n_grp = n_z * n_core
    rows, width = q_hbm.shape
    land_rows = land_hbm.shape[0]
    classes = lab_hbm.shape[1]
    tiles = n_lo * n_core
    loop = lax.axis_index("loop")
    grp = lax.axis_index("grp")
    hi, lo = loop // n_lo, lax.rem(loop, n_lo)
    z, core = grp // n_core, lax.rem(grp, n_core)

    def device(hi_, lo_, z_, core_):
        return (hi_ * n_lo + lo_, z_ * n_core + core_)

    def plus(a, d, n):
        return lax.rem(a + d + n, n)

    def remote(src, dst, send, recv, dev):
        return pltpu.make_async_remote_copy(
            src_ref=src, dst_ref=dst, send_sem=send, recv_sem=recv, device_id=dev, device_id_type=MESH
        )

    mine_q = hi * n_z + z
    mine_l = lo * n_core + core
    local = [
        pltpu.make_async_copy(q_hbm, q_all.at[mine_q], own_sem.at[0]),
        pltpu.make_async_copy(land_hbm, land_all.at[mine_l], own_sem.at[1]),
        pltpu.make_async_copy(lab_hbm, lab_all.at[mine_l], own_sem.at[2]),
    ]
    for c in local:
        c.start()

    peers = [(e, d) for e in range(n_hi) for d in range(n_z) if e or d]
    barrier = pltpu.get_barrier_semaphore()
    greet = [device(plus(hi, e, n_hi), lo, plus(z, d, n_z), core) for e, d in peers]
    greet += [device(hi, plus(lo, f, n_lo), z, core) for f in range(1, n_lo)]
    greet += [device(hi, lo, z, plus(core, s, n_core)) for s in range(1, n_core)]
    for dev in greet:
        pl.semaphore_signal(barrier, inc=1, device_id=dev, device_id_type=MESH)
    pl.semaphore_wait(barrier, len(greet))

    piece = land_rows // CHUNKS
    started = []

    def go(copy):
        copy.start()
        started.append(copy)

    def lx(src, slot, f, c):
        part_rows = pl.ds(c * piece, piece)
        return remote(
            src.at[part_rows],
            land_all.at[slot, part_rows],
            lx_send.at[f, c],
            lx_recv.at[f, c],
            device(hi, plus(lo, f, n_lo), z, core),
        )

    def bx(src, slot, f):
        return remote(
            src, lab_all.at[slot], bx_send.at[f], bx_recv.at[f], device(hi, plus(lo, f, n_lo), z, core)
        )

    def ls(src, slot, s, f, c):
        part_rows = pl.ds(c * piece, piece)
        return remote(
            src.at[part_rows],
            land_all.at[slot, part_rows],
            ls_send.at[s, f, c],
            ls_recv.at[s, f, c],
            device(hi, lo, z, plus(core, s, n_core)),
        )

    def bs(src, slot, s, f):
        return remote(
            src, lab_all.at[slot], bs_send.at[s, f], bs_recv.at[s, f], device(hi, lo, z, plus(core, s, n_core))
        )

    def qz(slot, d):
        return remote(
            q_hbm, q_all.at[slot], qz_send.at[d], qz_recv.at[d], device(hi, lo, plus(z, d, n_z), core)
        )

    def qy(src, slot, e, d):
        return remote(
            src, q_all.at[slot], qy_send.at[e, d], qy_recv.at[e, d], device(plus(hi, e, n_hi), lo, z, core)
        )

    for d in range(1, n_z):
        go(qz(mine_q, d))
    for f in range(1, n_lo):
        for c in range(CHUNKS):
            go(lx(land_hbm, mine_l, f, c))
        go(bx(lab_hbm, mine_l, f))
    for e in range(1, n_hi):
        go(qy(q_hbm, mine_q, e, 0))
    for s in range(1, n_core):
        for c in range(CHUNKS):
            go(ls(land_hbm, mine_l, s, 0, c))
        go(bs(lab_hbm, mine_l, s, 0))

    for d in range(1, n_z):
        slot = hi * n_z + plus(z, -d, n_z)
        qz(slot, d).wait_recv()
        for e in range(1, n_hi):
            go(qy(q_all.at[slot], slot, e, d))
    for f in range(1, n_lo):
        slot = plus(lo, -f, n_lo) * n_core + core
        for c in range(CHUNKS):
            lx(land_hbm, slot, f, c).wait_recv()
            for s in range(1, n_core):
                go(ls(land_all.at[slot], slot, s, f, c))
        bx(lab_hbm, slot, f).wait_recv()
        for s in range(1, n_core):
            go(bs(lab_all.at[slot], slot, s, f))
    for c in local:
        c.wait()
    for e in range(1, n_hi):
        for d in range(n_z):
            slot = plus(hi, -e, n_hi) * n_z + plus(z, -d, n_z)
            qy(q_hbm, slot, e, d).wait_recv()
    for f in range(n_lo):
        for s in range(1, n_core):
            slot = plus(lo, -f, n_lo) * n_core + plus(core, -s, n_core)
            for c in range(CHUNKS):
                ls(land_hbm, slot, s, f, c).wait_recv()
            bs(lab_hbm, slot, s, f).wait_recv()

    land = land_all[...].reshape(tiles * land_rows, width)
    labs = lab_all[...].reshape(tiles * land_rows, classes)
    land_f = land.astype(jnp.float32)
    square = land_f * land_f
    lanes = 128 if width % 128 == 0 else width
    folded = square[:, :lanes]
    for start in range(lanes, width, lanes):
        folded = folded + square[:, start : start + lanes]
    half_norm = 0.5 * jnp.sum(folded.T, axis=0, keepdims=True)
    scale_factor = 4.0 / math.sqrt(width)
    tile_of = lax.broadcasted_iota(jnp.int32, (1, tiles * land_rows), 1) // land_rows
    slab = n_z * rows
    lane = lax.broadcasted_iota(jnp.int32, (slab, classes), 1)

    def score(h, carry):
        flags = jnp.zeros((1, tiles * land_rows), jnp.int32)
        for t in range(tiles):
            source = (hi * n_lo + t // n_core) * n_grp + z * n_core + t % n_core
            flags = jnp.where(tile_of == t, mask_ref[h * n_lo + lo, source], flags)
        listed = flags > 0
        block = q_all[pl.ds(h * n_z, n_z)].reshape(slab, width)
        logits = lax.dot_general(
            block, land, (((1,), (1,)), ((), ())), preferred_element_type=jnp.float32
        )
        logits = (logits - half_norm) * scale_factor
        row_max = jnp.max(jnp.where(listed, logits, -1e30), axis=1, keepdims=True)
        weights = jnp.where(listed, jnp.exp(logits - row_max), 0.0)
        weight_sum = jnp.sum(weights, axis=1, keepdims=True)
        label_sum = jnp.dot(weights.astype(jnp.bfloat16), labs, preferred_element_type=jnp.float32)
        stats = jnp.zeros((slab, classes), jnp.float32)
        for i, term in enumerate(three_terms(row_max) + three_terms(weight_sum)):
            stats = jnp.where(lane == i, term, stats)
        message = jnp.concatenate([label_sum, stats], axis=1).astype(jnp.bfloat16)
        part[pl.ds(h * n_z, n_z)] = message.reshape(n_z, rows, 2 * classes)
        return carry

    lax.fori_loop(0, n_hi, score, 0, unroll=n_hi <= 4)

    def send_part(e, d, src, dst):
        return remote(
            part.at[src],
            got.at[dst],
            p_send.at[e, d],
            p_recv.at[e, d],
            device(plus(hi, e, n_hi), lo, plus(z, d, n_z), core),
        )

    for e, d in peers:
        go(send_part(e, d, plus(hi, e, n_hi) * n_z + plus(z, d, n_z), mine_q))
    got[mine_q] = part[mine_q]
    for e, d in peers:
        send_part(e, d, mine_q, plus(hi, -e, n_hi) * n_z + plus(z, -d, n_z)).wait_recv()

    parts = got[...].astype(jnp.float32)
    sums, stats = parts[:, :, :classes], parts[:, :, classes:]
    maxes = stats[:, :, 0:1] + stats[:, :, 1:2] + stats[:, :, 2:3]
    totals = stats[:, :, 3:4] + stats[:, :, 4:5] + stats[:, :, 5:6]
    keep = jnp.exp(maxes - jnp.max(maxes, axis=0, keepdims=True))
    out_ref[...] = jnp.sum(sums * keep, axis=0) / jnp.sum(totals * keep, axis=0)

    for copy in started:
        copy.wait_send()


def local(n_loop, n_grp, queries, landmarks, labels, tile_mask):
    n_lo = 2 if n_loop % 2 == 0 else 1
    n_core = 2 if n_grp % 2 == 0 else 1
    n_hi, n_z = n_loop // n_lo, n_grp // n_core
    rows, width = queries.shape
    land_rows, classes = labels.shape
    tiles = n_lo * n_core
    blocks = n_hi * n_z
    dma = pltpu.SemaphoreType.DMA
    any_space = pl.BlockSpec(memory_space=pl.ANY)
    scores = pl.pallas_call(
        functools.partial(kernel, (n_hi, n_lo, n_z, n_core)),
        out_shape=jax.ShapeDtypeStruct((rows, classes), jnp.float32),
        in_specs=[pl.BlockSpec(memory_space=pltpu.SMEM), any_space, any_space, any_space],
        out_specs=pl.BlockSpec(memory_space=pltpu.VMEM),
        scratch_shapes=[
            pltpu.VMEM((blocks, rows, width), jnp.bfloat16),
            pltpu.VMEM((tiles, land_rows, width), jnp.bfloat16),
            pltpu.VMEM((tiles, land_rows, classes), jnp.bfloat16),
            pltpu.VMEM((blocks, rows, 2 * classes), jnp.bfloat16),
            pltpu.VMEM((blocks, rows, 2 * classes), jnp.bfloat16),
            dma((3,)),
            dma((n_z,)),
            dma((n_z,)),
            dma((n_hi, n_z)),
            dma((n_hi, n_z)),
            dma((n_lo, CHUNKS)),
            dma((n_lo, CHUNKS)),
            dma((n_lo,)),
            dma((n_lo,)),
            dma((n_core, n_lo, CHUNKS)),
            dma((n_core, n_lo, CHUNKS)),
            dma((n_core, n_lo)),
            dma((n_core, n_lo)),
            dma((n_hi, n_z)),
            dma((n_hi, n_z)),
        ],
        compiler_params=pltpu.CompilerParams(
            collective_id=0, has_side_effects=True, vmem_limit_bytes=48 * 1024 * 1024
        ),
    )(tile_mask, queries, landmarks, labels)
    return scores.astype(jnp.bfloat16)


def solution(mesh):
    in_specs = (P(("loop", "grp"), None), P(("loop", "grp"), None), P(("loop", "grp"), None), P())
    out_specs = P(("loop", "grp"), None)
    body = functools.partial(local, mesh.shape["loop"], mesh.shape["grp"])
    return jax.shard_map(body, mesh=mesh, in_specs=in_specs, out_specs=out_specs, check_vma=False)
```

```python
import functools
import math

import jax
import jax.numpy as jnp
from jax import lax
from jax.experimental import pallas as pl
from jax.experimental.pallas import tpu as pltpu
from jax.sharding import PartitionSpec as P

MESH = pl.DeviceIdType.MESH
CHUNKS = 2


def three_terms(value):
    first = value.astype(jnp.bfloat16)
    rest = value - first.astype(jnp.float32)
    second = rest.astype(jnp.bfloat16)
    third = (rest - second.astype(jnp.float32)).astype(jnp.bfloat16)
    return [t.astype(jnp.float32) for t in (first, second, third)]


def kernel(
    dims,
    mask_hbm,
    q_hbm,
    land_hbm,
    lab_hbm,
    out_ref,
    mask_ref,
    fold,
    q_all,
    land_all,
    lab_all,
    part,
    got,
    own_sem,
    qz_send,
    qz_recv,
    qy_send,
    qy_recv,
    lx_send,
    lx_recv,
    bx_send,
    bx_recv,
    ls_send,
    ls_recv,
    bs_send,
    bs_recv,
    p_send,
    p_recv,
):
    n_hi, n_lo, n_z, n_core = dims
    n_grp = n_z * n_core
    rows, width = q_hbm.shape
    land_rows = land_hbm.shape[0]
    classes = lab_hbm.shape[1]
    tiles = n_lo * n_core
    loop = lax.axis_index("loop")
    grp = lax.axis_index("grp")
    hi, lo = loop // n_lo, lax.rem(loop, n_lo)
    z, core = grp // n_core, lax.rem(grp, n_core)

    def device(hi_, lo_, z_, core_):
        return (hi_ * n_lo + lo_, z_ * n_core + core_)

    def plus(a, d, n):
        return lax.rem(a + d + n, n)

    def remote(src, dst, send, recv, dev):
        return pltpu.make_async_remote_copy(
            src_ref=src, dst_ref=dst, send_sem=send, recv_sem=recv, device_id=dev, device_id_type=MESH
        )

    mine_q = hi * n_z + z
    mine_l = lo * n_core + core
    peers = [(e, d) for e in range(n_hi) for d in range(n_z) if e or d]
    barrier = pltpu.get_barrier_semaphore()
    greet = [device(plus(hi, e, n_hi), lo, plus(z, d, n_z), core) for e, d in peers]
    greet += [device(hi, plus(lo, f, n_lo), z, core) for f in range(1, n_lo)]
    greet += [device(hi, lo, z, plus(core, s, n_core)) for s in range(1, n_core)]
    for dev in greet:
        pl.semaphore_signal(barrier, inc=1, device_id=dev, device_id_type=MESH)
    local = [
        pltpu.make_async_copy(q_hbm, q_all.at[mine_q], own_sem.at[0]),
        pltpu.make_async_copy(land_hbm, land_all.at[mine_l], own_sem.at[1]),
        pltpu.make_async_copy(lab_hbm, lab_all.at[mine_l], own_sem.at[2]),
        pltpu.make_async_copy(mask_hbm, mask_ref, own_sem.at[3]),
    ]
    for c in local:
        c.start()
    pl.semaphore_wait(barrier, len(greet))

    piece = land_rows // CHUNKS
    started = []

    def go(copy):
        copy.start()
        started.append(copy)

    def square_sums(slot):
        land_f = land_all[slot].astype(jnp.float32)
        square = land_f * land_f
        lanes = fold.shape[2]
        total = square[:, :lanes]
        for start in range(lanes, width, lanes):
            total = total + square[:, start : start + lanes]
        fold[slot] = total

    def lx(src, slot, f, c):
        part_rows = pl.ds(c * piece, piece)
        return remote(
            src.at[part_rows],
            land_all.at[slot, part_rows],
            lx_send.at[f, c],
            lx_recv.at[f, c],
            device(hi, plus(lo, f, n_lo), z, core),
        )

    def bx(src, slot, f):
        return remote(
            src, lab_all.at[slot], bx_send.at[f], bx_recv.at[f], device(hi, plus(lo, f, n_lo), z, core)
        )

    def ls(src, slot, s, f, c):
        part_rows = pl.ds(c * piece, piece)
        return remote(
            src.at[part_rows],
            land_all.at[slot, part_rows],
            ls_send.at[s, f, c],
            ls_recv.at[s, f, c],
            device(hi, lo, z, plus(core, s, n_core)),
        )

    def bs(src, slot, s, f):
        return remote(
            src, lab_all.at[slot], bs_send.at[s, f], bs_recv.at[s, f], device(hi, lo, z, plus(core, s, n_core))
        )

    def qz(slot, d):
        return remote(
            q_hbm, q_all.at[slot], qz_send.at[d], qz_recv.at[d], device(hi, lo, plus(z, d, n_z), core)
        )

    def qy(src, slot, e, d):
        return remote(
            src, q_all.at[slot], qy_send.at[e, d], qy_recv.at[e, d], device(plus(hi, e, n_hi), lo, z, core)
        )

    for d in range(1, n_z):
        go(qz(mine_q, d))
    for f in range(1, n_lo):
        for c in range(CHUNKS):
            go(lx(land_hbm, mine_l, f, c))
        go(bx(lab_hbm, mine_l, f))
    for e in range(1, n_hi):
        go(qy(q_hbm, mine_q, e, 0))
    for s in range(1, n_core):
        for c in range(CHUNKS):
            go(ls(land_hbm, mine_l, s, 0, c))
        go(bs(lab_hbm, mine_l, s, 0))

    for c in local:
        c.wait()
    square_sums(mine_l)

    for d in range(1, n_z):
        slot = hi * n_z + plus(z, -d, n_z)
        qz(slot, d).wait_recv()
        for e in range(1, n_hi):
            go(qy(q_all.at[slot], slot, e, d))
    for f in range(1, n_lo):
        slot = plus(lo, -f, n_lo) * n_core + core
        for c in range(CHUNKS):
            lx(land_hbm, slot, f, c).wait_recv()
            for s in range(1, n_core):
                go(ls(land_all.at[slot], slot, s, f, c))
        bx(lab_hbm, slot, f).wait_recv()
        for s in range(1, n_core):
            go(bs(lab_all.at[slot], slot, s, f))
    for f in range(1, n_lo):
        square_sums(plus(lo, -f, n_lo) * n_core + core)
    for f in range(n_lo):
        for s in range(1, n_core):
            slot = plus(lo, -f, n_lo) * n_core + plus(core, -s, n_core)
            for c in range(CHUNKS):
                ls(land_hbm, slot, s, f, c).wait_recv()
            bs(lab_hbm, slot, s, f).wait_recv()
            square_sums(slot)
    for e in range(1, n_hi):
        for d in range(n_z):
            slot = plus(hi, -e, n_hi) * n_z + plus(z, -d, n_z)
            qy(q_hbm, slot, e, d).wait_recv()

    land = land_all[...].reshape(tiles * land_rows, width)
    labs = lab_all[...].reshape(tiles * land_rows, classes)
    half_norm = 0.5 * jnp.sum(fold[...].reshape(tiles * land_rows, -1).T, axis=0, keepdims=True)
    scale_factor = 4.0 / math.sqrt(width)
    tile_of = lax.broadcasted_iota(jnp.int32, (1, tiles * land_rows), 1) // land_rows
    slab = n_z * rows
    group = n_hi if n_hi <= 2 else 1
    lane = lax.broadcasted_iota(jnp.int32, (group * slab, classes), 1)
    row = lax.broadcasted_iota(jnp.int32, (group * slab, tiles * land_rows), 0)

    def score(step, carry):
        flags = jnp.zeros((group * slab, tiles * land_rows), jnp.int32)
        for i in range(group):
            of_row = jnp.zeros((1, tiles * land_rows), jnp.int32)
            for t in range(tiles):
                source = (hi * n_lo + t // n_core) * n_grp + z * n_core + t % n_core
                value = mask_ref[(step * group + i) * n_lo + lo, source]
                of_row = jnp.where(tile_of == t, value, of_row)
            flags = jnp.where(row >= i * slab, of_row, flags)
        listed = flags > 0
        here = pl.ds(step * (group * n_z), group * n_z)
        block = q_all[here].reshape(group * slab, width)
        logits = lax.dot_general(
            block, land, (((1,), (1,)), ((), ())), preferred_element_type=jnp.float32
        )
        logits = (logits - half_norm) * scale_factor
        row_max = jnp.max(jnp.where(listed, logits, -1e30), axis=1, keepdims=True)
        weights = jnp.where(listed, jnp.exp(logits - row_max), 0.0)
        weight_sum = jnp.sum(weights, axis=1, keepdims=True)
        label_sum = jnp.dot(weights.astype(jnp.bfloat16), labs, preferred_element_type=jnp.float32)
        stats = jnp.zeros((group * slab, classes), jnp.float32)
        for i, term in enumerate(three_terms(row_max) + three_terms(weight_sum)):
            stats = jnp.where(lane == i, term, stats)
        message = jnp.concatenate([label_sum, stats], axis=1).astype(jnp.bfloat16)
        part[here] = message.reshape(group * n_z, rows, 2 * classes)
        return carry

    lax.fori_loop(0, n_hi // group, score, 0)

    def send_part(e, d, src, dst):
        return remote(
            part.at[src],
            got.at[dst],
            p_send.at[e, d],
            p_recv.at[e, d],
            device(plus(hi, e, n_hi), lo, plus(z, d, n_z), core),
        )

    for e, d in peers:
        go(send_part(e, d, plus(hi, e, n_hi) * n_z + plus(z, d, n_z), mine_q))
    got[mine_q] = part[mine_q]
    for e, d in peers:
        send_part(e, d, mine_q, plus(hi, -e, n_hi) * n_z + plus(z, -d, n_z)).wait_recv()

    parts = got[...].astype(jnp.float32)
    sums, stats = parts[:, :, :classes], parts[:, :, classes:]
    maxes = stats[:, :, 0:1] + stats[:, :, 1:2] + stats[:, :, 2:3]
    totals = stats[:, :, 3:4] + stats[:, :, 4:5] + stats[:, :, 5:6]
    keep = jnp.exp(maxes - jnp.max(maxes, axis=0, keepdims=True))
    out_ref[...] = jnp.sum(sums * keep, axis=0) / jnp.sum(totals * keep, axis=0)

    for copy in started:
        copy.wait_send()


def local(n_loop, n_grp, queries, landmarks, labels, tile_mask):
    n_lo = 2 if n_loop % 2 == 0 else 1
    n_core = 2 if n_grp % 2 == 0 else 1
    n_hi, n_z = n_loop // n_lo, n_grp // n_core
    rows, width = queries.shape
    land_rows, classes = labels.shape
    tiles = n_lo * n_core
    blocks = n_hi * n_z
    lanes = 128 if width % 128 == 0 else width
    dma = pltpu.SemaphoreType.DMA
    any_space = pl.BlockSpec(memory_space=pltpu.HBM)
    scores = pl.pallas_call(
        functools.partial(kernel, (n_hi, n_lo, n_z, n_core)),
        out_shape=jax.ShapeDtypeStruct((rows, classes), jnp.float32),
        in_specs=[any_space] * 4,
        out_specs=pl.BlockSpec(memory_space=pltpu.VMEM),
        scratch_shapes=[
            pltpu.SMEM(tile_mask.shape, jnp.int32),
            pltpu.VMEM((tiles, land_rows, lanes), jnp.float32),
            pltpu.VMEM((blocks, rows, width), jnp.bfloat16),
            pltpu.VMEM((tiles, land_rows, width), jnp.bfloat16),
            pltpu.VMEM((tiles, land_rows, classes), jnp.bfloat16),
            pltpu.VMEM((blocks, rows, 2 * classes), jnp.bfloat16),
            pltpu.VMEM((blocks, rows, 2 * classes), jnp.bfloat16),
            dma((4,)),
            dma((n_z,)),
            dma((n_z,)),
            dma((n_hi, n_z)),
            dma((n_hi, n_z)),
            dma((n_lo, CHUNKS)),
            dma((n_lo, CHUNKS)),
            dma((n_lo,)),
            dma((n_lo,)),
            dma((n_core, n_lo, CHUNKS)),
            dma((n_core, n_lo, CHUNKS)),
            dma((n_core, n_lo)),
            dma((n_core, n_lo)),
            dma((n_hi, n_z)),
            dma((n_hi, n_z)),
        ],
        compiler_params=pltpu.CompilerParams(
            collective_id=0, has_side_effects=True, vmem_limit_bytes=60 * 1024 * 1024
        ),
    )(tile_mask, queries, landmarks, labels)
    return scores.astype(jnp.bfloat16)


def solution(mesh):
    in_specs = (P(("loop", "grp"), None), P(("loop", "grp"), None), P(("loop", "grp"), None), P())
    out_specs = P(("loop", "grp"), None)
    body = functools.partial(local, mesh.shape["loop"], mesh.shape["grp"])
    return jax.shard_map(body, mesh=mesh, in_specs=in_specs, out_specs=out_specs, check_vma=False)
```

```python
import functools
import math

import jax
import jax.numpy as jnp
from jax import lax
from jax.experimental import pallas as pl
from jax.experimental.pallas import tpu as pltpu
from jax.sharding import PartitionSpec as P

MESH = pl.DeviceIdType.MESH
CHUNKS = 1


def three_terms(value):
    first = value.astype(jnp.bfloat16)
    rest = value - first.astype(jnp.float32)
    second = rest.astype(jnp.bfloat16)
    third = (rest - second.astype(jnp.float32)).astype(jnp.bfloat16)
    return [t.astype(jnp.float32) for t in (first, second, third)]


def kernel(
    dims,
    mask_hbm,
    q_hbm,
    land_hbm,
    lab_hbm,
    out_ref,
    mask_ref,
    fold,
    q_all,
    land_all,
    lab_all,
    part,
    got,
    own_sem,
    qz_send,
    qz_recv,
    qy_send,
    qy_recv,
    lx_send,
    lx_recv,
    bx_send,
    bx_recv,
    ls_send,
    ls_recv,
    bs_send,
    bs_recv,
    p_send,
    p_recv,
):
    n_hi, n_lo, n_z, n_core = dims
    n_grp = n_z * n_core
    rows, width = q_hbm.shape
    land_rows = land_hbm.shape[0]
    classes = lab_hbm.shape[1]
    tiles = n_lo * n_core
    loop = lax.axis_index("loop")
    grp = lax.axis_index("grp")
    hi, lo = loop // n_lo, lax.rem(loop, n_lo)
    z, core = grp // n_core, lax.rem(grp, n_core)

    def device(hi_, lo_, z_, core_):
        return (hi_ * n_lo + lo_, z_ * n_core + core_)

    def plus(a, d, n):
        return lax.rem(a + d + n, n)

    def partner(a, d, n, sign):
        if n & (n - 1):
            return plus(a, sign * d, n)
        for bit in range(n.bit_length()):
            if d >> bit & 1:
                a = a + (1 << bit) * (1 - 2 * lax.rem(a // (1 << bit), 2))
        return a

    def z_to(d):
        return partner(z, d, n_z, 1)

    def z_from(d):
        return partner(z, d, n_z, -1)

    def remote(src, dst, send, recv, dev):
        return pltpu.make_async_remote_copy(
            src_ref=src, dst_ref=dst, send_sem=send, recv_sem=recv, device_id=dev, device_id_type=MESH
        )

    mine_q = hi * n_z + z
    mine_l = lo * n_core + core
    peers = [(e, d) for d in reversed(range(n_z)) for e in reversed(range(n_hi)) if e or d]
    barrier = pltpu.get_barrier_semaphore()
    greet = [device(hi, lo, z_to(d), core) for d in reversed(range(1, n_z))]
    greet += [device(plus(hi, e, n_hi), lo, z, core) for e in range(1, n_hi)]
    greet += [device(hi, plus(lo, f, n_lo), z, core) for f in range(1, n_lo)]
    greet += [device(hi, lo, z, plus(core, s, n_core)) for s in range(1, n_core)]
    for dev in greet:
        pl.semaphore_signal(barrier, inc=1, device_id=dev, device_id_type=MESH)
    local = [
        pltpu.make_async_copy(q_hbm, q_all.at[mine_q], own_sem.at[0]),
        pltpu.make_async_copy(land_hbm, land_all.at[mine_l], own_sem.at[1]),
        pltpu.make_async_copy(lab_hbm, lab_all.at[mine_l], own_sem.at[2]),
        pltpu.make_async_copy(mask_hbm, mask_ref, own_sem.at[3]),
    ]
    for c in local:
        c.start()
    pl.semaphore_wait(barrier, len(greet))

    piece = land_rows // CHUNKS
    started = []

    def go(copy):
        copy.start()
        started.append(copy)

    def square_sums(slot):
        land_f = land_all[slot].astype(jnp.float32)
        square = land_f * land_f
        lanes = fold.shape[2]
        total = square[:, :lanes]
        for start in range(lanes, width, lanes):
            total = total + square[:, start : start + lanes]
        fold[slot] = total

    def lx(src, slot, f, c):
        part_rows = pl.ds(c * piece, piece)
        return remote(
            src.at[part_rows],
            land_all.at[slot, part_rows],
            lx_send.at[f, c],
            lx_recv.at[f, c],
            device(hi, plus(lo, f, n_lo), z, core),
        )

    def bx(src, slot, f):
        return remote(
            src, lab_all.at[slot], bx_send.at[f], bx_recv.at[f], device(hi, plus(lo, f, n_lo), z, core)
        )

    def ls(src, slot, s, f, c):
        part_rows = pl.ds(c * piece, piece)
        return remote(
            src.at[part_rows],
            land_all.at[slot, part_rows],
            ls_send.at[s, f, c],
            ls_recv.at[s, f, c],
            device(hi, lo, z, plus(core, s, n_core)),
        )

    def bs(src, slot, s, f):
        return remote(
            src, lab_all.at[slot], bs_send.at[s, f], bs_recv.at[s, f], device(hi, lo, z, plus(core, s, n_core))
        )

    def qz(slot, d):
        return remote(
            q_hbm, q_all.at[slot], qz_send.at[d], qz_recv.at[d], device(hi, lo, z_to(d), core)
        )

    def qy(src, slot, e, d):
        return remote(
            src, q_all.at[slot], qy_send.at[e, d], qy_recv.at[e, d], device(plus(hi, e, n_hi), lo, z, core)
        )

    for d in reversed(range(1, n_z)):
        go(qz(mine_q, d))
    for f in range(1, n_lo):
        for c in range(CHUNKS):
            go(lx(land_hbm, mine_l, f, c))
        go(bx(lab_hbm, mine_l, f))
    for e in range(1, n_hi):
        go(qy(q_hbm, mine_q, e, 0))
    for s in range(1, n_core):
        for c in range(CHUNKS):
            go(ls(land_hbm, mine_l, s, 0, c))
        go(bs(lab_hbm, mine_l, s, 0))

    for c in local:
        c.wait()
    square_sums(mine_l)

    for d in range(1, n_z):
        slot = hi * n_z + z_from(d)
        qz(slot, d).wait_recv()
        for e in range(1, n_hi):
            go(qy(q_all.at[slot], slot, e, d))
    for f in range(1, n_lo):
        slot = plus(lo, -f, n_lo) * n_core + core
        for c in range(CHUNKS):
            lx(land_hbm, slot, f, c).wait_recv()
            for s in range(1, n_core):
                go(ls(land_all.at[slot], slot, s, f, c))
        bx(lab_hbm, slot, f).wait_recv()
        for s in range(1, n_core):
            go(bs(lab_all.at[slot], slot, s, f))
    for f in range(1, n_lo):
        square_sums(plus(lo, -f, n_lo) * n_core + core)
    for f in range(n_lo):
        for s in range(1, n_core):
            slot = plus(lo, -f, n_lo) * n_core + plus(core, -s, n_core)
            for c in range(CHUNKS):
                ls(land_hbm, slot, s, f, c).wait_recv()
            bs(lab_hbm, slot, s, f).wait_recv()
            square_sums(slot)
    for e in range(1, n_hi):
        for d in range(n_z):
            slot = plus(hi, -e, n_hi) * n_z + z_from(d)
            qy(q_hbm, slot, e, d).wait_recv()

    land = land_all[...].reshape(tiles * land_rows, width)
    labs = lab_all[...].reshape(tiles * land_rows, classes)
    half_norm = 0.5 * jnp.sum(fold[...].reshape(tiles * land_rows, -1).T, axis=0, keepdims=True)
    scale_factor = 4.0 / math.sqrt(width)
    tile_of = lax.broadcasted_iota(jnp.int32, (1, tiles * land_rows), 1) // land_rows
    slab = n_z * rows
    group = n_hi if n_hi <= 2 else 1
    lane = lax.broadcasted_iota(jnp.int32, (group * slab, classes), 1)
    row = lax.broadcasted_iota(jnp.int32, (group * slab, tiles * land_rows), 0)

    def score(step, carry):
        flags = jnp.zeros((group * slab, tiles * land_rows), jnp.int32)
        for i in range(group):
            of_row = jnp.zeros((1, tiles * land_rows), jnp.int32)
            for t in range(tiles):
                source = (hi * n_lo + t // n_core) * n_grp + z * n_core + t % n_core
                value = mask_ref[(step * group + i) * n_lo + lo, source]
                of_row = jnp.where(tile_of == t, value, of_row)
            flags = jnp.where(row >= i * slab, of_row, flags)
        listed = flags > 0
        here = pl.ds(step * (group * n_z), group * n_z)
        block = q_all[here].reshape(group * slab, width)
        logits = lax.dot_general(
            block, land, (((1,), (1,)), ((), ())), preferred_element_type=jnp.float32
        )
        logits = (logits - half_norm) * scale_factor
        row_max = jnp.max(jnp.where(listed, logits, -1e30), axis=1, keepdims=True)
        weights = jnp.where(listed, jnp.exp(logits - row_max), 0.0)
        weight_sum = jnp.sum(weights, axis=1, keepdims=True)
        label_sum = jnp.dot(weights.astype(jnp.bfloat16), labs, preferred_element_type=jnp.float32)
        stats = jnp.zeros((group * slab, classes), jnp.float32)
        for i, term in enumerate(three_terms(row_max) + three_terms(weight_sum)):
            stats = jnp.where(lane == i, term, stats)
        message = jnp.concatenate([label_sum, stats], axis=1).astype(jnp.bfloat16)
        part[here] = message.reshape(group * n_z, rows, 2 * classes)
        return carry

    lax.fori_loop(0, n_hi // group, score, 0)

    def send_part(e, d, src, dst):
        return remote(
            part.at[src],
            got.at[dst],
            p_send.at[e, d],
            p_recv.at[e, d],
            device(plus(hi, e, n_hi), lo, z_to(d), core),
        )

    for e, d in peers:
        go(send_part(e, d, plus(hi, e, n_hi) * n_z + z_to(d), mine_q))
    got[mine_q] = part[mine_q]
    for e, d in peers:
        send_part(e, d, mine_q, plus(hi, -e, n_hi) * n_z + z_from(d)).wait_recv()

    parts = got[...].astype(jnp.float32)
    sums, stats = parts[:, :, :classes], parts[:, :, classes:]
    maxes = stats[:, :, 0:1] + stats[:, :, 1:2] + stats[:, :, 2:3]
    totals = stats[:, :, 3:4] + stats[:, :, 4:5] + stats[:, :, 5:6]
    keep = jnp.exp(maxes - jnp.max(maxes, axis=0, keepdims=True))
    out_ref[...] = jnp.sum(sums * keep, axis=0) / jnp.sum(totals * keep, axis=0)

    for copy in started:
        copy.wait_send()


def local(n_loop, n_grp, queries, landmarks, labels, tile_mask):
    n_lo = 2 if n_loop % 2 == 0 else 1
    n_core = 2 if n_grp % 2 == 0 else 1
    n_hi, n_z = n_loop // n_lo, n_grp // n_core
    rows, width = queries.shape
    land_rows, classes = labels.shape
    tiles = n_lo * n_core
    blocks = n_hi * n_z
    lanes = 128 if width % 128 == 0 else width
    dma = pltpu.SemaphoreType.DMA
    any_space = pl.BlockSpec(memory_space=pltpu.HBM)
    scores = pl.pallas_call(
        functools.partial(kernel, (n_hi, n_lo, n_z, n_core)),
        out_shape=jax.ShapeDtypeStruct((rows, classes), jnp.float32),
        in_specs=[any_space] * 4,
        out_specs=pl.BlockSpec(memory_space=pltpu.VMEM),
        scratch_shapes=[
            pltpu.SMEM(tile_mask.shape, jnp.int32),
            pltpu.VMEM((tiles, land_rows, lanes), jnp.float32),
            pltpu.VMEM((blocks, rows, width), jnp.bfloat16),
            pltpu.VMEM((tiles, land_rows, width), jnp.bfloat16),
            pltpu.VMEM((tiles, land_rows, classes), jnp.bfloat16),
            pltpu.VMEM((blocks, rows, 2 * classes), jnp.bfloat16),
            pltpu.VMEM((blocks, rows, 2 * classes), jnp.bfloat16),
            dma((4,)),
            dma((n_z,)),
            dma((n_z,)),
            dma((n_hi, n_z)),
            dma((n_hi, n_z)),
            dma((n_lo, CHUNKS)),
            dma((n_lo, CHUNKS)),
            dma((n_lo,)),
            dma((n_lo,)),
            dma((n_core, n_lo, CHUNKS)),
            dma((n_core, n_lo, CHUNKS)),
            dma((n_core, n_lo)),
            dma((n_core, n_lo)),
            dma((n_hi, n_z)),
            dma((n_hi, n_z)),
        ],
        compiler_params=pltpu.CompilerParams(
            collective_id=0, has_side_effects=True, vmem_limit_bytes=60 * 1024 * 1024
        ),
    )(tile_mask, queries, landmarks, labels)
    return scores.astype(jnp.bfloat16)


def solution(mesh):
    in_specs = (P(("loop", "grp"), None), P(("loop", "grp"), None), P(("loop", "grp"), None), P())
    out_specs = P(("loop", "grp"), None)
    body = functools.partial(local, mesh.shape["loop"], mesh.shape["grp"])
    return jax.shard_map(body, mesh=mesh, in_specs=in_specs, out_specs=out_specs, check_vma=False)
```

```python
import functools
import math

import jax
import jax.numpy as jnp
from jax import lax
from jax.experimental import pallas as pl
from jax.experimental.pallas import tpu as pltpu
from jax.sharding import PartitionSpec as P

MESH = pl.DeviceIdType.MESH
CHUNKS = 1


def three_terms(value):
    first = value.astype(jnp.bfloat16)
    rest = value - first.astype(jnp.float32)
    second = rest.astype(jnp.bfloat16)
    third = (rest - second.astype(jnp.float32)).astype(jnp.bfloat16)
    return [t.astype(jnp.float32) for t in (first, second, third)]


def kernel(
    dims,
    mask_hbm,
    q_hbm,
    land_hbm,
    lab_hbm,
    out_ref,
    mask_ref,
    fold,
    q_all,
    land_all,
    lab_all,
    part,
    got,
    own_sem,
    qz_send,
    qz_recv,
    qy_send,
    qy_recv,
    lx_send,
    lx_recv,
    bx_send,
    bx_recv,
    ls_send,
    ls_recv,
    bs_send,
    bs_recv,
    p_send,
    p_recv,
):
    n_hi, n_lo, n_z, n_core = dims
    n_grp = n_z * n_core
    rows, width = q_hbm.shape
    land_rows = land_hbm.shape[0]
    classes = lab_hbm.shape[1]
    tiles = n_lo * n_core
    loop = lax.axis_index("loop")
    grp = lax.axis_index("grp")
    hi, lo = loop // n_lo, lax.rem(loop, n_lo)
    z, core = grp // n_core, lax.rem(grp, n_core)

    def device(hi_, lo_, z_, core_):
        return (hi_ * n_lo + lo_, z_ * n_core + core_)

    def plus(a, d, n):
        return lax.rem(a + d + n, n)

    def partner(a, d, n, sign):
        if n & (n - 1):
            return plus(a, sign * d, n)
        for bit in range(n.bit_length()):
            if d >> bit & 1:
                a = a + (1 << bit) * (1 - 2 * lax.rem(a // (1 << bit), 2))
        return a

    def z_to(d):
        return partner(z, d, n_z, 1)

    def z_from(d):
        return partner(z, d, n_z, -1)

    def remote(src, dst, send, recv, dev):
        return pltpu.make_async_remote_copy(
            src_ref=src, dst_ref=dst, send_sem=send, recv_sem=recv, device_id=dev, device_id_type=MESH
        )

    mine_q = hi * n_z + z
    mine_l = lo * n_core + core
    peers = [(e, d) for d in reversed(range(n_z)) for e in reversed(range(n_hi)) if e or d]
    barrier = pltpu.get_barrier_semaphore()
    greet = [device(hi, lo, z_to(d), core) for d in reversed(range(1, n_z))]
    greet += [device(plus(hi, e, n_hi), lo, z, core) for e in range(1, n_hi)]
    greet += [device(hi, plus(lo, f, n_lo), z, core) for f in range(1, n_lo)]
    greet += [device(hi, lo, z, plus(core, s, n_core)) for s in range(1, n_core)]
    for dev in greet:
        pl.semaphore_signal(barrier, inc=1, device_id=dev, device_id_type=MESH)
    local = [
        pltpu.make_async_copy(q_hbm, q_all.at[mine_q], own_sem.at[0]),
        pltpu.make_async_copy(land_hbm, land_all.at[mine_l], own_sem.at[1]),
        pltpu.make_async_copy(lab_hbm, lab_all.at[mine_l], own_sem.at[2]),
        pltpu.make_async_copy(mask_hbm, mask_ref, own_sem.at[3]),
    ]
    for c in local:
        c.start()
    pl.semaphore_wait(barrier, len(greet))

    piece = land_rows // CHUNKS
    started = []

    def go(copy):
        copy.start()
        started.append(copy)

    def square_sums(slot):
        land_f = land_all[slot].astype(jnp.float32)
        square = land_f * land_f
        lanes = fold.shape[2]
        total = square[:, :lanes]
        for start in range(lanes, width, lanes):
            total = total + square[:, start : start + lanes]
        fold[slot] = total

    def lx(src, slot, f, c):
        part_rows = pl.ds(c * piece, piece)
        return remote(
            src.at[part_rows],
            land_all.at[slot, part_rows],
            lx_send.at[f, c],
            lx_recv.at[f, c],
            device(hi, plus(lo, f, n_lo), z, core),
        )

    def bx(src, slot, f):
        return remote(
            src, lab_all.at[slot], bx_send.at[f], bx_recv.at[f], device(hi, plus(lo, f, n_lo), z, core)
        )

    def ls(src, slot, s, f, c):
        part_rows = pl.ds(c * piece, piece)
        return remote(
            src.at[part_rows],
            land_all.at[slot, part_rows],
            ls_send.at[s, f, c],
            ls_recv.at[s, f, c],
            device(hi, lo, z, plus(core, s, n_core)),
        )

    def bs(src, slot, s, f):
        return remote(
            src, lab_all.at[slot], bs_send.at[s, f], bs_recv.at[s, f], device(hi, lo, z, plus(core, s, n_core))
        )

    def qz(slot, d):
        return remote(
            q_hbm, q_all.at[slot], qz_send.at[d], qz_recv.at[d], device(hi, lo, z_to(d), core)
        )

    def qy(src, slot, e, d):
        return remote(
            src, q_all.at[slot], qy_send.at[e, d], qy_recv.at[e, d], device(plus(hi, e, n_hi), lo, z, core)
        )

    for d in range(1, n_z):
        go(qz(mine_q, d))
    for f in range(1, n_lo):
        for c in range(CHUNKS):
            go(lx(land_hbm, mine_l, f, c))
        go(bx(lab_hbm, mine_l, f))
    for e in range(1, n_hi):
        go(qy(q_hbm, mine_q, e, 0))
    for s in range(1, n_core):
        for c in range(CHUNKS):
            go(ls(land_hbm, mine_l, s, 0, c))
        go(bs(lab_hbm, mine_l, s, 0))

    for c in local:
        c.wait()
    square_sums(mine_l)

    for d in range(1, n_z):
        slot = hi * n_z + z_from(d)
        qz(slot, d).wait_recv()
        for e in range(1, n_hi):
            go(qy(q_all.at[slot], slot, e, d))
    for f in range(1, n_lo):
        slot = plus(lo, -f, n_lo) * n_core + core
        for c in range(CHUNKS):
            lx(land_hbm, slot, f, c).wait_recv()
            for s in range(1, n_core):
                go(ls(land_all.at[slot], slot, s, f, c))
        bx(lab_hbm, slot, f).wait_recv()
        for s in range(1, n_core):
            go(bs(lab_all.at[slot], slot, s, f))
    for f in range(1, n_lo):
        square_sums(plus(lo, -f, n_lo) * n_core + core)
    for f in range(n_lo):
        for s in range(1, n_core):
            slot = plus(lo, -f, n_lo) * n_core + plus(core, -s, n_core)
            for c in range(CHUNKS):
                ls(land_hbm, slot, s, f, c).wait_recv()
            bs(lab_hbm, slot, s, f).wait_recv()
            square_sums(slot)
    for e in range(1, n_hi):
        for d in range(n_z):
            slot = plus(hi, -e, n_hi) * n_z + z_from(d)
            qy(q_hbm, slot, e, d).wait_recv()

    land = land_all[...].reshape(tiles * land_rows, width)
    labs = lab_all[...].reshape(tiles * land_rows, classes)
    half_norm = 0.5 * jnp.sum(fold[...].reshape(tiles * land_rows, -1).T, axis=0, keepdims=True)
    scale_factor = 4.0 / math.sqrt(width)
    tile_of = lax.broadcasted_iota(jnp.int32, (1, tiles * land_rows), 1) // land_rows
    slab = n_z * rows
    group = n_hi if n_hi <= 2 else 1
    lane = lax.broadcasted_iota(jnp.int32, (group * slab, classes), 1)
    row = lax.broadcasted_iota(jnp.int32, (group * slab, tiles * land_rows), 0)

    def score(step, carry):
        flags = jnp.zeros((group * slab, tiles * land_rows), jnp.int32)
        for i in range(group):
            of_row = jnp.zeros((1, tiles * land_rows), jnp.int32)
            for t in range(tiles):
                source = (hi * n_lo + t // n_core) * n_grp + z * n_core + t % n_core
                value = mask_ref[(step * group + i) * n_lo + lo, source]
                of_row = jnp.where(tile_of == t, value, of_row)
            flags = jnp.where(row >= i * slab, of_row, flags)
        listed = flags > 0
        here = pl.ds(step * (group * n_z), group * n_z)
        block = q_all[here].reshape(group * slab, width)
        logits = lax.dot_general(
            block, land, (((1,), (1,)), ((), ())), preferred_element_type=jnp.float32
        )
        logits = (logits - half_norm) * scale_factor
        row_max = jnp.max(jnp.where(listed, logits, -1e30), axis=1, keepdims=True)
        weights = jnp.where(listed, jnp.exp(logits - row_max), 0.0)
        weight_sum = jnp.sum(weights, axis=1, keepdims=True)
        label_sum = jnp.dot(weights.astype(jnp.bfloat16), labs, preferred_element_type=jnp.float32)
        stats = jnp.zeros((group * slab, classes), jnp.float32)
        for i, term in enumerate(three_terms(row_max) + three_terms(weight_sum)):
            stats = jnp.where(lane == i, term, stats)
        message = jnp.concatenate([label_sum, stats], axis=1).astype(jnp.bfloat16)
        part[here] = message.reshape(group * n_z, rows, 2 * classes)
        return carry

    lax.fori_loop(0, n_hi // group, score, 0)

    def send_part(e, d, src, dst):
        return remote(
            part.at[src],
            got.at[dst],
            p_send.at[e, d],
            p_recv.at[e, d],
            device(plus(hi, e, n_hi), lo, z_to(d), core),
        )

    for e, d in peers:
        go(send_part(e, d, plus(hi, e, n_hi) * n_z + z_to(d), mine_q))
    got[mine_q] = part[mine_q]
    for e, d in peers:
        send_part(e, d, mine_q, plus(hi, -e, n_hi) * n_z + z_from(d)).wait_recv()

    parts = got[...].astype(jnp.float32)
    sums, stats = parts[:, :, :classes], parts[:, :, classes:]
    maxes = stats[:, :, 0:1] + stats[:, :, 1:2] + stats[:, :, 2:3]
    totals = stats[:, :, 3:4] + stats[:, :, 4:5] + stats[:, :, 5:6]
    keep = jnp.exp(maxes - jnp.max(maxes, axis=0, keepdims=True))
    out_ref[...] = jnp.sum(sums * keep, axis=0) / jnp.sum(totals * keep, axis=0)

    for copy in started:
        copy.wait_send()


def local(n_loop, n_grp, queries, landmarks, labels, tile_mask):
    n_lo = 2 if n_loop % 2 == 0 else 1
    n_core = 2 if n_grp % 2 == 0 else 1
    n_hi, n_z = n_loop // n_lo, n_grp // n_core
    rows, width = queries.shape
    land_rows, classes = labels.shape
    tiles = n_lo * n_core
    blocks = n_hi * n_z
    lanes = 128 if width % 128 == 0 else width
    dma = pltpu.SemaphoreType.DMA
    any_space = pl.BlockSpec(memory_space=pltpu.HBM)
    scores = pl.pallas_call(
        functools.partial(kernel, (n_hi, n_lo, n_z, n_core)),
        out_shape=jax.ShapeDtypeStruct((rows, classes), jnp.float32),
        in_specs=[any_space] * 4,
        out_specs=pl.BlockSpec(memory_space=pltpu.VMEM),
        scratch_shapes=[
            pltpu.SMEM(tile_mask.shape, jnp.int32),
            pltpu.VMEM((tiles, land_rows, lanes), jnp.float32),
            pltpu.VMEM((blocks, rows, width), jnp.bfloat16),
            pltpu.VMEM((tiles, land_rows, width), jnp.bfloat16),
            pltpu.VMEM((tiles, land_rows, classes), jnp.bfloat16),
            pltpu.VMEM((blocks, rows, 2 * classes), jnp.bfloat16),
            pltpu.VMEM((blocks, rows, 2 * classes), jnp.bfloat16),
            dma((4,)),
            dma((n_z,)),
            dma((n_z,)),
            dma((n_hi, n_z)),
            dma((n_hi, n_z)),
            dma((n_lo, CHUNKS)),
            dma((n_lo, CHUNKS)),
            dma((n_lo,)),
            dma((n_lo,)),
            dma((n_core, n_lo, CHUNKS)),
            dma((n_core, n_lo, CHUNKS)),
            dma((n_core, n_lo)),
            dma((n_core, n_lo)),
            dma((n_hi, n_z)),
            dma((n_hi, n_z)),
        ],
        compiler_params=pltpu.CompilerParams(
            collective_id=0, has_side_effects=True, vmem_limit_bytes=60 * 1024 * 1024
        ),
    )(tile_mask, queries, landmarks, labels)
    return scores.astype(jnp.bfloat16)


def solution(mesh):
    in_specs = (P(("loop", "grp"), None), P(("loop", "grp"), None), P(("loop", "grp"), None), P())
    out_specs = P(("loop", "grp"), None)
    body = functools.partial(local, mesh.shape["loop"], mesh.shape["grp"])
    return jax.shard_map(body, mesh=mesh, in_specs=in_specs, out_specs=out_specs, check_vma=False)
```
